32 devices in a mesh: node: 16 (over z, y, x), local: 2 (over core).
Axes of the slice: x: 2, y: 2, z: 4, core: 2. Of those that a mesh axis runs over, the one named last changes fastest.
Arguments:
- grad_out: bfloat16 [2048, 7168], P('node', 'local'), may hold values from -6 to 6
- probs: bfloat16 [2048, 8], P('node'), may hold values from 0.099609375 to 2.5
- node_list: int32 [2048, 4], P('node'), may hold values from 0 to 15, all different within a row; in each aligned block of 128 rows (0 to 127, 128 to 255, ...) at most 48 rows name the same one
- weight_down: bfloat16 [32, 1024, 7168], P('node', 'local'), may hold values from -0.1875 to 0.1875
- saved_hidden: bfloat16 [32, 768, 1024], P('node', None, 'local'), may hold values from -0.1875 to 0.1875
Outputs:
- grad_hidden: bfloat16 [32, 768, 1024], P('node', None, 'local')
- grad_probs: float32 [2048, 8], P('node')
The draws below stay inside these ranges and needn't reach their ends.
Inputs may be any that keep to these rules, and one draw needn't show every extreme that they name: `node_list`: each token lists 4 different nodes. Among the 128 tokens of one index of node, at most 48 list any one node, and some node is listed by exactly 48 of them.
All inputs are finite; a program needn't handle non-finite values.
Results may differ from the reference program's by a relative error of at most 0.001.
Values may be sent and summed in bfloat16 or wider, within the bound.
A program may use at most 128 MiB of HBM per device.

```python
import math
import jax
import jax.numpy as jnp
import numpy as np
from jax import lax

D = 7168
FF = 1024
EXP_NODE = 2
MAXNODE = 4
TOPK = 8
TOK_NODE = 128
CAP = 48
TOKENS = 2048
EXPERTS = 32
N_NODE = 16


def block_levels(stream_key, dims, cuts, least, high):
    loudness, own = 1.0, jax.random.fold_in(stream_key, 6)
    for position, parts in cuts:
        steps = jnp.exp(jax.random.uniform(jax.random.fold_in(own, position), (parts,), jnp.float32, least / len(cuts), high / len(cuts)))
        loudness = loudness * jnp.repeat(steps, dims[position] // parts).reshape([-1 if axis == position else 1 for axis in range(len(dims))])
    return loudness


def deal_out(own_key, own, number, rows, number_of, top, limit, skew):
    order = jax.random.permutation(own_key, number_of)
    crowded, ordinary = portions_of(number_of, rows * top, limit, skew, True), portions_of(number_of, rows * top, limit, skew, False)
    places = jnp.arange(number_of)

    def named(sizes, offset_by):
        used = int((sizes > 0).sum())
        fixed = max(1, used // 4)
        moved = fixed + (places - fixed + offset_by * (used - fixed)) % max(1, number_of - fixed)
        return jnp.zeros((number_of,), jnp.int32).at[order[jnp.where(places < fixed, places, moved)]].set(jnp.asarray(sizes, jnp.int32))

    sizes = jnp.where(number % 4 == 0, named(crowded, number // 4), named(ordinary, number - number // 4 - 1))
    mixed = jax.random.permutation(jax.random.fold_in(own, 3), number_of)
    donor, receiver = mixed[0:number_of // 2 * 2:2], mixed[1:number_of // 2 * 2:2]
    margin = jnp.minimum(sizes[donor] - 1, limit - sizes[receiver]) // 2
    margin = jnp.where((donor == order[0]) | (receiver == order[0]) | (sizes[receiver] == 0), 0, jnp.maximum(margin, 0))
    moved = jax.random.randint(jax.random.fold_in(own, 4), (number_of // 2,), 0, 1 << 20) % (margin + 1)
    sizes = sizes.at[donor].add(-moved).at[receiver].add(moved)
    members = jnp.searchsorted(jnp.cumsum(sizes), jnp.arange(rows * top), side="right").astype(jnp.int32)
    listing = members.reshape(top, rows).T
    listing = listing[jax.random.permutation(jax.random.fold_in(own, 1), rows)]
    offset_by = jax.random.randint(jax.random.fold_in(own, 2), (rows, 1), 0, top)
    return jnp.take_along_axis(listing, (jnp.arange(top)[None, :] + offset_by) % top, axis=1)


def portions_of(count, total, bound, skew, full):
    loads = [(1 << 20) // math.isqrt(grade ** skew) + 1 for grade in range(1, count + 1)]
    largest = bound if full else min(bound, max(-(-total // count), total * loads[0] // sum(loads)))
    least = 1 if total - largest >= count - 1 else 0
    given, surplus = [largest] + [least] * (count - 1), total - largest - least * (count - 1)
    while surplus > 0:
        movable = [i for i in range(1, count) if given[i] < largest] or [i for i in range(1, count) if given[i] < bound]
        mass, remaining = sum([loads[i] for i in movable]), surplus
        for i in movable:
            addition = min(bound - given[i], max(1, remaining * loads[i] // mass), surplus)
            given[i] = given[i] + addition
            surplus = surplus - addition
    return np.array(given)


def normal_values(rng, dims, width, limit, split=(), held_as=jnp.bfloat16):
    loudness = block_levels(rng, dims, split, -0.22, 0.18) if split else 1.0
    entries = jax.random.normal(rng, dims, jnp.float32) * width * loudness
    return jnp.minimum(jnp.maximum(entries, -limit), limit).astype(held_as)


def setup_inputs(seed: int = 0) -> dict:
    splits = jax.random.split(jax.random.key(seed), 6)
    grad_out = normal_values(splits[0], (TOKENS, D), 1.0, 6.0, ((0, 16), (1, 2)))
    probs = jnp.clip(jnp.exp(math.log(2.5) - 3.2227897 * jax.random.uniform(splits[1], (TOKENS, TOPK), jnp.float32) ** block_levels(splits[1], (TOKENS, TOPK), ((0, 16),), -0.2, 0.2)), 0.099609375, 2.5).astype(jnp.bfloat16)
    node_list_keys = jax.random.split(jax.random.fold_in(splits[2], 1), TOKENS // TOK_NODE)
    node_list_turns = jax.random.permutation(jax.random.fold_in(splits[2], 3), TOKENS // TOK_NODE)
    node_list = jax.vmap(lambda own, number: deal_out(jax.random.fold_in(splits[2], 2), own, number, TOK_NODE, N_NODE, MAXNODE, CAP, 2))(node_list_keys, node_list_turns).reshape((TOKENS, MAXNODE))
    weight_down = normal_values(splits[3], (EXPERTS, FF, D), FF ** -0.5, 0.1875, ((0, 16), (1, 2)))
    saved_hidden = normal_values(splits[4], (EXPERTS, N_NODE * CAP, FF), 0.03, 0.1875, ((0, 16), (2, 2)))
    return {"grad_out": grad_out, "probs": probs, "node_list": node_list, "weight_down": weight_down, "saved_hidden": saved_hidden}


def reference(grad_out, probs, node_list, weight_down, saved_hidden):
    listed = node_list.reshape(N_NODE, TOK_NODE, MAXNODE)
    node_ids = jnp.arange(N_NODE, dtype=jnp.int32)
    member = jnp.sum((listed[..., None] == node_ids).astype(jnp.int32), axis=2)
    arrival = jnp.cumsum(member, axis=1) - member
    slot_pos = jnp.take_along_axis(arrival, listed, axis=2).astype(jnp.int32)
    source_ids = jnp.broadcast_to(jnp.arange(N_NODE, dtype=jnp.int32)[:, None, None], listed.shape)
    token_ids = source_ids * TOK_NODE + jnp.arange(TOK_NODE, dtype=jnp.int32)[None, :, None]
    choice_ids = jnp.broadcast_to(jnp.arange(MAXNODE, dtype=jnp.int32)[None, None, :], listed.shape)
    table_token = jnp.full((N_NODE, N_NODE, CAP), TOKENS, jnp.int32).at[listed, source_ids, slot_pos].set(token_ids)
    table_choice = jnp.zeros((N_NODE, N_NODE, CAP), jnp.int32).at[listed, source_ids, slot_pos].set(choice_ids)

    def one_expert(expert):
        home = expert // EXP_NODE
        which = expert % EXP_NODE
        tokens_here = table_token[home].reshape(-1)
        valid = tokens_here < TOKENS
        safe_index = jnp.minimum(tokens_here, TOKENS - 1)
        rows = jnp.where(valid[:, None], grad_out[safe_index], jnp.zeros((), grad_out.dtype))
        grads = jnp.dot(rows, weight_down[expert].T, preferred_element_type=jnp.float32)
        column = (EXP_NODE * table_choice[home].reshape(-1) + which).astype(jnp.int32)
        weights = jnp.where(valid, probs[safe_index, column].astype(jnp.float32), jnp.zeros((), jnp.float32))
        hidden = (weights[:, None] * grads).astype(jnp.bfloat16)
        scores = jnp.sum(saved_hidden[expert].astype(jnp.float32) * grads, axis=1)
        return hidden, scores, column

    grad_hidden, scores, columns = lax.map(one_expert, jnp.arange(EXPERTS, dtype=jnp.int32))
    token_index = jnp.repeat(table_token.reshape(N_NODE, -1), EXP_NODE, axis=0)
    grad_probs = jnp.zeros((TOKENS, TOPK), jnp.float32).at[token_index, columns].set(scores, mode="drop")
    return grad_hidden, grad_probs
```

```python
import functools

import jax
import jax.numpy as jnp
from jax import lax
from jax.experimental import pallas as pl
from jax.experimental.pallas import tpu as pltpu
from jax.sharding import PartitionSpec as P

MESH = pl.DeviceIdType.MESH
PLANES = 4
SIDE = 4
F32 = jnp.float32
BF16 = jnp.bfloat16
NT = (((1,), (1,)), ((), ()))


def gather_slots(source, source_row, slot_valid):
    padded = jnp.concatenate([source, jnp.zeros((1, source.shape[1]), source.dtype)], axis=0)
    index = jnp.where(slot_valid, source_row, source.shape[0])
    return jnp.take(padded, index, axis=0)


def plain(grad_out, probs, node_list, weight_down, saved_hidden):
    node_count = lax.axis_size("node")
    tok_rows = node_list.shape[0]
    route_count = node_list.shape[1]
    slot_rows = saved_hidden.shape[1]
    capacity = slot_rows // node_count
    expert_count = weight_down.shape[0]
    node_ids = lax.broadcasted_iota(jnp.int32, (tok_rows, route_count, node_count), 2)
    listed = (node_list[:, :, None] == node_ids).astype(jnp.float32)
    member = jnp.sum((node_list[:, :, None] == node_ids).astype(jnp.int32), axis=1)
    arrival = jnp.cumsum(member, axis=0) - member
    positions = lax.broadcasted_iota(jnp.int32, (tok_rows, node_count, capacity), 2)
    select_mask = (arrival[:, :, None] == positions) & (member[:, :, None] == 1)
    select_count = select_mask.astype(jnp.int32)
    token_iota = lax.broadcasted_iota(jnp.int32, (tok_rows, node_count, capacity), 0)
    source_row = jnp.sum(select_count * token_iota, axis=0)
    slot_valid = jnp.sum(select_count, axis=0) > 0
    select_full = select_mask.astype(jnp.float32)
    grouped = probs.reshape(tok_rows, route_count, expert_count).astype(jnp.float32)
    picked = jnp.einsum("tjm,tjc->tmc", listed, grouped, precision=lax.Precision.HIGHEST)
    prob_send = jnp.einsum(
        "tms,tmc->msc", select_full, picked, precision=lax.Precision.HIGHEST
    ).astype(jnp.bfloat16)
    rows_send = gather_slots(grad_out, source_row, slot_valid)
    rows_in, prob_in = (
        lax.all_to_all(rows_send, "node", split_axis=0, concat_axis=0, tiled=True),
        lax.all_to_all(prob_send, "node", split_axis=0, concat_axis=0, tiled=True),
    )
    rows_in = lax.all_gather(rows_in.reshape(slot_rows, -1), "local", axis=1, tiled=True)
    hidden_grads = jnp.einsum(
        "rd,ehd->erh", rows_in, weight_down, preferred_element_type=jnp.float32
    )
    scales = jnp.transpose(prob_in.reshape(slot_rows, expert_count).astype(jnp.float32))
    grad_hidden = (scales[:, :, None] * hidden_grads).astype(jnp.bfloat16)
    partial_value = jnp.sum(saved_hidden.astype(jnp.float32) * hidden_grads, axis=2)
    partial_value = jnp.transpose(partial_value).reshape(node_count, capacity, expert_count)
    summed = lax.psum(partial_value, "local")
    returned = lax.all_to_all(summed, "node", split_axis=0, concat_axis=0, tiled=True)
    per_node = jnp.einsum("tms,msc->tmc", select_full, returned, precision=lax.Precision.HIGHEST)
    grad_probs = jnp.einsum("tjm,tmc->tjc", listed, per_node, precision=lax.Precision.HIGHEST)
    return (grad_hidden, grad_probs.reshape(tok_rows, route_count * expert_count))


def fused_kernel(
    chunks, go_ref, pr_ref, nl_ref, w_ref, sh_ref, out_ref, gp_ref,
    zbuf, aux, auxf, smat, sbuf, psend, rbuf, pbuf, wv, hv, acc, obuf, part, ret, home, onehot,
    in_sem, w_sem, h_sem, o_sem, z_recv, z_up, z_down, a_recv, a_up, a_down,
    r_send, r_recv, p_send, p_recv, s_send, s_recv, t_send, t_recv,
):
    node, core = lax.axis_index("node"), lax.axis_index("local")
    z, q = node // SIDE, node % SIDE
    x, y = q % 2, q // 2
    cap, width = rbuf.shape[4], rbuf.shape[5]
    toks = zbuf.shape[2]
    hid = hv.shape[3]
    units = PLANES * chunks
    other = 1 - core
    total = PLANES * SIDE * 2
    me = node * 2 + core

    barrier = pltpu.get_barrier_semaphore()

    def greet(i, carry):
        peer = (me + i) % total
        pl.semaphore_signal(barrier, inc=1, device_id=(peer // 2, peer % 2), device_id_type=MESH)
        return carry

    lax.fori_loop(1, total, greet, 0)

    def load_in(ch):
        return pltpu.make_async_copy(go_ref.at[:, pl.ds(ch * width, width)], zbuf.at[z, ch], in_sem.at[ch])

    def load_w(h, ch):
        return pltpu.make_async_copy(
            w_ref.at[:, pl.ds((h * chunks + ch) * width, width)], wv.at[h, ch], w_sem.at[h, ch]
        )

    load_h = pltpu.make_async_copy(sh_ref, hv, h_sem)
    for ch in range(chunks):
        load_in(ch).start()
    for ch in range(chunks):
        for h in range(2):
            load_w(h, ch).start()
    load_h.start()

    nodes = PLANES * SIDE
    rows_m = lax.broadcasted_iota(jnp.int32, (nodes, toks), 0)
    member = jnp.zeros((nodes, toks), F32)
    first = jnp.zeros((nodes, toks), F32)
    second = jnp.zeros((nodes, toks), F32)
    hits = []
    for j in range(4):
        hit = (nl_ref[j:j + 1, :] == rows_m).astype(F32)
        hits.append(hit)
        member = member + hit
        first = first + hit * pr_ref[2 * j:2 * j + 1, :].astype(F32)
        second = second + hit * pr_ref[2 * j + 1:2 * j + 2, :].astype(F32)
    before = (
        lax.broadcasted_iota(jnp.int32, (toks, toks), 0) < lax.broadcasted_iota(jnp.int32, (toks, toks), 1)
    ).astype(F32).astype(BF16)
    arrival = jnp.dot(member.astype(BF16), before, preferred_element_type=F32)
    slot_of = jnp.where(member > 0.5, arrival, -1.0)
    aux[z] = jnp.concatenate([slot_of, first, second], axis=0).astype(BF16)
    tall = jnp.concatenate(
        [nl_ref[...].astype(F32)]
        + [jnp.sum(hits[j] * slot_of, axis=0, keepdims=True) for j in range(4)]
        + [jnp.zeros((toks - 8, toks), F32)],
        axis=0,
    ).T
    home[...] = tall
    lane = lax.broadcasted_iota(jnp.int32, (toks, toks), 1)
    lane_node = (lane % nodes).astype(F32)
    for j in range(4):
        onehot[j] = jnp.where((lane < 3 * nodes) & (tall[:, j:j + 1] == lane_node), 1.0, 0.0).astype(BF16)

    pl.semaphore_wait(barrier, total - 1)

    def unit(u):
        k0, c0 = u // chunks, u % chunks
        v = u - chunks
        mixed = ((z == 1) | (z == 2)) & (k0 >= 1) & (k0 <= 2)
        k = jnp.where(mixed, 1 + v % 2, k0)
        ch = jnp.where(mixed, v // 2, c0)
        near = z + 1 - 2 * (z % 2)
        low = z < 2
        zb = jnp.where(
            k == 0, z, jnp.where(k == 1, near, jnp.where(k == 2, jnp.where(low, 2, 1), jnp.where(low, 3, 0)))
        )
        return k, ch, zb

    def mate(d):
        return (x + d % 2) % 2 + 2 * ((y + d // 2) % 2)

    def along(ref, index, send, recv, step):
        return pltpu.make_async_remote_copy(
            src_ref=ref.at[index], dst_ref=ref.at[index], send_sem=send.at[index], recv_sem=recv.at[index],
            device_id=(node + step * SIDE, core), device_id_type=MESH,
        )

    def hop(zb, ch, step):
        return along(zbuf, (zb, ch), z_up if step > 0 else z_down, z_recv, step)

    def hop_aux(zb, step):
        return along(aux, zb, a_up if step > 0 else a_down, a_recv, step)

    def pack(zb, ch, d):
        return pltpu.make_async_remote_copy(
            src_ref=sbuf.at[zb, ch, d - 1], dst_ref=rbuf.at[core, ch, zb, q],
            send_sem=r_send.at[zb, ch, d - 1], recv_sem=r_recv.at[zb, ch, d - 1],
            device_id=(z * SIDE + mate(d), core), device_id_type=MESH,
        )

    def pack_in(zb, ch, d):
        return pltpu.make_async_remote_copy(
            src_ref=sbuf.at[zb, ch, d - 1], dst_ref=rbuf.at[core, ch, zb, mate(d)],
            send_sem=r_send.at[zb, ch, d - 1], recv_sem=r_recv.at[zb, ch, d - 1],
            device_id=(z * SIDE + mate(d), core), device_id_type=MESH,
        )

    def scale(zb, d):
        return pltpu.make_async_remote_copy(
            src_ref=psend.at[zb, d - 1], dst_ref=pbuf.at[zb, q],
            send_sem=p_send.at[zb, d - 1], recv_sem=p_recv.at[zb, d - 1],
            device_id=(z * SIDE + mate(d), core), device_id_type=MESH,
        )

    def scale_in(zb, d):
        return pltpu.make_async_remote_copy(
            src_ref=psend.at[zb, d - 1], dst_ref=pbuf.at[zb, mate(d)],
            send_sem=p_send.at[zb, d - 1], recv_sem=p_recv.at[zb, d - 1],
            device_id=(z * SIDE + mate(d), core), device_id_type=MESH,
        )

    def share(half, zb, ch):
        return pltpu.make_async_remote_copy(
            src_ref=rbuf.at[half, ch, zb], dst_ref=rbuf.at[half, ch, zb],
            send_sem=s_send.at[zb, ch], recv_sem=s_recv.at[zb, ch],
            device_id=(node, other), device_id_type=MESH,
        )

    def give(zb, d, dc):
        target = zb * SIDE + mate(d)
        return pltpu.make_async_remote_copy(
            src_ref=part.at[zb, d], dst_ref=ret.at[node, core],
            send_sem=t_send.at[zb, d, dc], recv_sem=t_recv.at[node, core],
            device_id=(target, (core + dc) % 2), device_id_type=MESH,
        )

    def give_in(m, c):
        return pltpu.make_async_remote_copy(
            src_ref=part.at[0, 0], dst_ref=ret.at[m, c],
            send_sem=t_send.at[0, 0, 0], recv_sem=t_recv.at[m, c],
            device_id=(node, other), device_id_type=MESH,
        )

    def store(zb, e):
        return pltpu.make_async_copy(obuf.at[zb, e], out_ref.at[e, zb], o_sem.at[zb, e])

    cap_rows = lax.broadcasted_iota(jnp.int32, (cap, toks), 0).astype(F32)
    cap_lane = lax.broadcasted_iota(jnp.int32, (cap, 128), 1)

    def stage_a(u):
        k, ch, zb = unit(u)

        @pl.when(k == 0)
        def _():
            load_in(ch).wait()

        @pl.when(k > 0)
        def _():
            @pl.when(ch == 0)
            def _():
                hop_aux(zb, 1).wait_recv()

            hop(zb, ch, 1).wait_recv()

        for step, go in ((1, (zb <= z) & (z < PLANES - 1)), (-1, (zb >= z) & (z > 0))):
            @pl.when(go)
            def _(step=step):
                @pl.when(ch == 0)
                def _():
                    hop_aux(zb, step).start()

                hop(zb, ch, step).start()

        @pl.when(ch == 0)
        def _():
            auxf[...] = aux[zb].astype(F32)
            for d in (3, 1, 2, 0):
                m = z * SIDE + mate(d)
                sel = (auxf[pl.ds(m, 1), :] == cap_rows).astype(F32)
                smat[zb, d] = sel.astype(BF16)
                col0 = jnp.sum(sel * auxf[pl.ds(nodes + m, 1), :], axis=1, keepdims=True)
                col1 = jnp.sum(sel * auxf[pl.ds(2 * nodes + m, 1), :], axis=1, keepdims=True)
                value = jnp.where(cap_lane == 0, col0, jnp.where(cap_lane == 1, col1, 0.0)).astype(BF16)
                if d:
                    psend[zb, d - 1] = value
                    scale(zb, d).start()
                else:
                    pbuf[zb, q] = value

        for d in (3, 1, 2, 0):
            value = jnp.dot(smat[zb, d], zbuf[zb, ch], preferred_element_type=F32).astype(BF16)
            if d:
                sbuf[zb, ch, d - 1] = value
                pack(zb, ch, d).start()
            else:
                rbuf[core, ch, zb, q] = value

    def stage_b(u):
        k, ch, zb = unit(u)
        for d in (1, 2, 3):
            pack_in(zb, ch, d).wait_recv()

        share(core, zb, ch).start()

    def stage_c(u):
        k, ch, zb = unit(u)
        share(other, zb, ch).wait_recv()

        @pl.when(ch == 0)
        def _():
            acc[zb] = jnp.zeros(acc.shape[1:], F32)

        left = rbuf[0, ch, zb].reshape(SIDE * cap, width)
        right = rbuf[1, ch, zb].reshape(SIDE * cap, width)
        tile = min(256, hid)
        for n in range(2 * hid // tile):
            cols = slice(n * tile, (n + 1) * tile)
            acc[zb, :, cols] += (
                lax.dot_general(left, wv[0, ch, cols, :], NT, preferred_element_type=F32)
                + lax.dot_general(right, wv[1, ch, cols, :], NT, preferred_element_type=F32)
            )

        @pl.when(ch == chunks - 1)
        def _():
            for d in (1, 2, 3):
                scale_in(zb, d).wait_recv()
            scales = pbuf[zb].reshape(SIDE * cap, 128).astype(F32)
            folded = []
            for e in range(2):
                g = acc[zb, :, e * hid:(e + 1) * hid]
                prod = hv[e, zb].astype(F32) * g
                fold = prod[:, :128]
                for b in range(1, hid // 128):
                    fold = fold + prod[:, b * 128:(b + 1) * 128]
                folded.append(fold)
                obuf[zb, e] = (scales[:, e:e + 1] * g).astype(BF16)
                store(zb, e).start()
            fill = jnp.zeros((128 - 2 * cap, 128), F32)
            for s in range(SIDE):
                rows = slice(s * cap, (s + 1) * cap)
                sums = jnp.sum(
                    jnp.concatenate([folded[0][rows], folded[1][rows], fill], axis=0).T, axis=0, keepdims=True
                )
                for d in range(SIDE):
                    @pl.when(mate(d) == s)
                    def _(d=d, sums=sums):
                        part[zb, d] = jnp.broadcast_to(sums, (8, 128))
            for d in range(SIDE):
                for dc in range(2):
                    if d == 0 and dc == 0:
                        @pl.when(zb != z)
                        def _():
                            give(zb, 0, 0).start()

                        @pl.when(zb == z)
                        def _():
                            ret[node, core] = part[zb, 0]
                    else:
                        give(zb, d, dc).start()

    def body(it, carry):
        @pl.when(it < units)
        def _():
            stage_a(it)

        @pl.when(it == 2)
        def _():
            for ch in range(chunks):
                for h in range(2):
                    load_w(h, ch).wait()
            load_h.wait()

        @pl.when(it >= 2)
        def _():
            stage_c(it - 2)

        @pl.when((it >= 1) & (it <= units))
        def _():
            stage_b(it - 1)

        return carry

    lax.fori_loop(0, units + 2, body, 0)

    def finish_block(zb, carry):
        for e in range(2):
            store(zb, e).wait()
        for step, go in ((1, (zb <= z) & (z < PLANES - 1)), (-1, (zb >= z) & (z > 0))):
            @pl.when(go)
            def _(step=step):
                hop_aux(zb, step).wait_send()

        for d in range(1, SIDE):
            scale(zb, d).wait_send()
        for d in range(SIDE):
            for dc in range(2):
                if d == 0 and dc == 0:
                    @pl.when(zb != z)
                    def _():
                        give(zb, 0, 0).wait_send()
                else:
                    give(zb, d, dc).wait_send()

        def finish_unit(ch, inner):
            for step, go in ((1, (zb <= z) & (z < PLANES - 1)), (-1, (zb >= z) & (z > 0))):
                @pl.when(go)
                def _(step=step):
                    hop(zb, ch, step).wait_send()

            for d in range(1, SIDE):
                pack(zb, ch, d).wait_send()
            share(core, zb, ch).wait_send()
            return inner

        return lax.fori_loop(0, chunks, finish_unit, carry)

    lax.fori_loop(0, PLANES, finish_block, 0)

    def arrive(i, carry):
        peer = (me + i) % total
        give_in(peer // 2, peer % 2).wait_recv()
        return carry

    lax.fori_loop(1, total, arrive, 0)

    sub = lax.broadcasted_iota(jnp.int32, (8, 128), 0)
    halves = []
    for base in range(0, nodes, 8):
        rows = jnp.zeros((8, 128), F32)
        for m in range(8):
            rows = jnp.where(sub == m, ret[base + m, 0] + ret[base + m, 1], rows)
        halves.append(rows)
    sums = jnp.concatenate(halves, axis=0)
    high = sums.astype(BF16).astype(F32)
    rest = sums - high
    middle = rest.astype(BF16).astype(F32)
    parts = jnp.concatenate(
        [high, middle, rest - middle, jnp.zeros((128 - 3 * nodes, 128), F32)], axis=0
    ).astype(BF16)
    lanes = lax.broadcasted_iota(jnp.int32, (toks, 128), 1)
    lanes_f = lanes.astype(F32)
    result = jnp.zeros((toks, 128), F32)
    for j in range(4):
        picked = jnp.dot(onehot[j], parts, preferred_element_type=F32)
        slot = home[:, 4 + j:5 + j]
        for e in range(2):
            column = jnp.sum(jnp.where(lanes_f == slot + float(e * cap), picked, 0.0), axis=1, keepdims=True)
            result = jnp.where(lanes == 2 * j + e, column, result)
    gp_ref[...] = result.T[:8, :]


def fused(chunks, grad_out, probs, node_list, weight_down, saved_hidden):
    toks, half = grad_out.shape
    width = half // chunks
    experts, hid, full = weight_down.shape
    slots = saved_hidden.shape[1]
    cap = slots // (PLANES * SIDE)
    group = SIDE * cap
    dma = pltpu.SemaphoreType.DMA
    anywhere = pl.BlockSpec(memory_space=pl.ANY)
    vmem = pl.BlockSpec(memory_space=pltpu.VMEM)
    out, gp = pl.pallas_call(
        functools.partial(fused_kernel, chunks),
        out_shape=(
            jax.ShapeDtypeStruct((experts, PLANES, group, hid), BF16),
            jax.ShapeDtypeStruct((8, toks), F32),
        ),
        in_specs=[anywhere, vmem, vmem, anywhere, anywhere],
        out_specs=(anywhere, vmem),
        scratch_shapes=[
            pltpu.VMEM((PLANES, chunks, toks, width), BF16),
            pltpu.VMEM((PLANES, 48, toks), BF16),
            pltpu.VMEM((48, toks), F32),
            pltpu.VMEM((PLANES, SIDE, cap, toks), BF16),
            pltpu.VMEM((PLANES, chunks, 3, cap, width), BF16),
            pltpu.VMEM((PLANES, 3, cap, 128), BF16),
            pltpu.VMEM((2, chunks, PLANES, SIDE, cap, width), BF16),
            pltpu.VMEM((PLANES, SIDE, cap, 128), BF16),
            pltpu.VMEM((2, chunks, experts * hid, width), BF16),
            pltpu.VMEM((experts, PLANES, group, hid), BF16),
            pltpu.VMEM((PLANES, group, experts * hid), F32),
            pltpu.VMEM((PLANES, experts, group, hid), BF16),
            pltpu.VMEM((PLANES, SIDE, 8, 128), F32),
            pltpu.VMEM((PLANES * SIDE, 2, 8, 128), F32),
            pltpu.VMEM((toks, toks), F32),
            pltpu.VMEM((4, toks, toks), BF16),
            dma((chunks,)),
            dma((2, chunks)),
            dma(()),
            dma((PLANES, 2)),
            dma((PLANES, chunks)),
            dma((PLANES, chunks)),
            dma((PLANES, chunks)),
            dma((PLANES,)),
            dma((PLANES,)),
            dma((PLANES,)),
            dma((PLANES, chunks, 3)),
            dma((PLANES, chunks, 3)),
            dma((PLANES, 3)),
            dma((PLANES, 3)),
            dma((PLANES, chunks)),
            dma((PLANES, chunks)),
            dma((PLANES, SIDE, 2)),
            dma((PLANES * SIDE, 2)),
        ],
        compiler_params=pltpu.CompilerParams(
            collective_id=0, has_side_effects=True, vmem_limit_bytes=56 * 2**20
        ),
        cost_estimate=pl.CostEstimate(
            flops=2 * slots * full * experts * hid, bytes_accessed=2 * experts * hid * full, transcendentals=0
        ),
    )(
        grad_out,
        probs.T,
        node_list.T,
        weight_down.reshape(experts * hid, full),
        saved_hidden.reshape(experts, PLANES, group, hid),
    )
    return out.reshape(experts, slots, hid), gp.T


def on_device(*args):
    grad_out, probs, node_list, weight_down, saved_hidden = args
    nodes, cores = lax.axis_size("node"), lax.axis_size("local")
    cap = saved_hidden.shape[1] // nodes
    suits = (
        nodes == PLANES * SIDE
        and cores == 2
        and cap % 16 == 0
        and 2 * cap <= 128
        and node_list.shape == (128, 4)
        and weight_down.shape[0] == 2
        and weight_down.shape[1] % 128 == 0
        and grad_out.shape[1] % 512 == 0
    )
    if suits:
        return fused(4, *args)
    return plain(*args)


def solution(mesh):
    return jax.shard_map(
        on_device,
        mesh=mesh,
        in_specs=(
            P("node", "local"),
            P("node", None),
            P("node", None),
            P("node", "local", None),
            P("node", None, "local"),
        ),
        out_specs=(P("node", None, "local"), P("node", None)),
        check_vma=False,
    )
```

```python
import functools

import jax
import jax.numpy as jnp
from jax import lax
from jax.experimental import pallas as pl
from jax.experimental.pallas import tpu as pltpu
from jax.sharding import PartitionSpec as P

MESH = pl.DeviceIdType.MESH
PLANES = 4
SIDE = 4
F32 = jnp.float32
BF16 = jnp.bfloat16
NT = (((1,), (1,)), ((), ()))


def gather_slots(source, source_row, slot_valid):
    padded = jnp.concatenate([source, jnp.zeros((1, source.shape[1]), source.dtype)], axis=0)
    index = jnp.where(slot_valid, source_row, source.shape[0])
    return jnp.take(padded, index, axis=0)


def plain(grad_out, probs, node_list, weight_down, saved_hidden):
    node_count = lax.axis_size("node")
    tok_rows = node_list.shape[0]
    route_count = node_list.shape[1]
    slot_rows = saved_hidden.shape[1]
    capacity = slot_rows // node_count
    expert_count = weight_down.shape[0]
    node_ids = lax.broadcasted_iota(jnp.int32, (tok_rows, route_count, node_count), 2)
    listed = (node_list[:, :, None] == node_ids).astype(jnp.float32)
    member = jnp.sum((node_list[:, :, None] == node_ids).astype(jnp.int32), axis=1)
    arrival = jnp.cumsum(member, axis=0) - member
    positions = lax.broadcasted_iota(jnp.int32, (tok_rows, node_count, capacity), 2)
    select_mask = (arrival[:, :, None] == positions) & (member[:, :, None] == 1)
    select_count = select_mask.astype(jnp.int32)
    token_iota = lax.broadcasted_iota(jnp.int32, (tok_rows, node_count, capacity), 0)
    source_row = jnp.sum(select_count * token_iota, axis=0)
    slot_valid = jnp.sum(select_count, axis=0) > 0
    select_full = select_mask.astype(jnp.float32)
    grouped = probs.reshape(tok_rows, route_count, expert_count).astype(jnp.float32)
    picked = jnp.einsum("tjm,tjc->tmc", listed, grouped, precision=lax.Precision.HIGHEST)
    prob_send = jnp.einsum(
        "tms,tmc->msc", select_full, picked, precision=lax.Precision.HIGHEST
    ).astype(jnp.bfloat16)
    rows_send = gather_slots(grad_out, source_row, slot_valid)
    rows_in, prob_in = (
        lax.all_to_all(rows_send, "node", split_axis=0, concat_axis=0, tiled=True),
        lax.all_to_all(prob_send, "node", split_axis=0, concat_axis=0, tiled=True),
    )
    rows_in = lax.all_gather(rows_in.reshape(slot_rows, -1), "local", axis=1, tiled=True)
    hidden_grads = jnp.einsum(
        "rd,ehd->erh", rows_in, weight_down, preferred_element_type=jnp.float32
    )
    scales = jnp.transpose(prob_in.reshape(slot_rows, expert_count).astype(jnp.float32))
    grad_hidden = (scales[:, :, None] * hidden_grads).astype(jnp.bfloat16)
    partial_value = jnp.sum(saved_hidden.astype(jnp.float32) * hidden_grads, axis=2)
    partial_value = jnp.transpose(partial_value).reshape(node_count, capacity, expert_count)
    summed = lax.psum(partial_value, "local")
    returned = lax.all_to_all(summed, "node", split_axis=0, concat_axis=0, tiled=True)
    per_node = jnp.einsum("tms,msc->tmc", select_full, returned, precision=lax.Precision.HIGHEST)
    grad_probs = jnp.einsum("tjm,tmc->tjc", listed, per_node, precision=lax.Precision.HIGHEST)
    return (grad_hidden, grad_probs.reshape(tok_rows, route_count * expert_count))


def fused_kernel(
    chunks, go_ref, pr_ref, nl_ref, w_ref, sh_ref, out_ref, gp_ref,
    zbuf, aux, auxf, smat, sbuf, psend, rbuf, pbuf, wv, hv, acc, obuf, part, ret, home, onehot,
    in_sem, w_sem, h_sem, o_sem, z_recv, z_up, z_down, a_recv, a_up, a_down,
    r_send, r_recv, p_send, p_recv, s_send, s_recv, t_send, t_recv,
):
    node, core = lax.axis_index("node"), lax.axis_index("local")
    z, q = node // SIDE, node % SIDE
    x, y = q % 2, q // 2
    cap, width = rbuf.shape[4], rbuf.shape[5]
    toks = zbuf.shape[2]
    hid = hv.shape[3]
    units = PLANES * chunks
    other = 1 - core
    total = PLANES * SIDE * 2
    me = node * 2 + core

    barrier = pltpu.get_barrier_semaphore()

    def greet(i, carry):
        peer = (me + i) % total
        pl.semaphore_signal(barrier, inc=1, device_id=(peer // 2, peer % 2), device_id_type=MESH)
        return carry

    lax.fori_loop(1, total, greet, 0)

    def load_in(ch):
        return pltpu.make_async_copy(go_ref.at[:, pl.ds(ch * width, width)], zbuf.at[z, ch], in_sem.at[ch])

    def load_w(h, ch):
        return pltpu.make_async_copy(
            w_ref.at[:, pl.ds((h * chunks + ch) * width, width)], wv.at[ch, :, pl.ds(h * width, width)],
            w_sem.at[h, ch],
        )

    load_h = pltpu.make_async_copy(sh_ref, hv, h_sem)
    for ch in range(chunks):
        load_in(ch).start()
    for ch in range(chunks):
        for h in range(2):
            load_w(h, ch).start()
    load_h.start()

    nodes = PLANES * SIDE
    rows_m = lax.broadcasted_iota(jnp.int32, (nodes, toks), 0)
    member = jnp.zeros((nodes, toks), F32)
    first = jnp.zeros((nodes, toks), F32)
    second = jnp.zeros((nodes, toks), F32)
    hits = []
    for j in range(4):
        hit = (nl_ref[j:j + 1, :] == rows_m).astype(F32)
        hits.append(hit)
        member = member + hit
        first = first + hit * pr_ref[2 * j:2 * j + 1, :].astype(F32)
        second = second + hit * pr_ref[2 * j + 1:2 * j + 2, :].astype(F32)
    before = (
        lax.broadcasted_iota(jnp.int32, (toks, toks), 0) < lax.broadcasted_iota(jnp.int32, (toks, toks), 1)
    ).astype(F32).astype(BF16)
    arrival = jnp.dot(member.astype(BF16), before, preferred_element_type=F32)
    slot_of = jnp.where(member > 0.5, arrival, -1.0)
    aux[z] = jnp.concatenate([slot_of, first, second], axis=0).astype(BF16)
    tall = jnp.concatenate(
        [nl_ref[...].astype(F32)]
        + [jnp.sum(hits[j] * slot_of, axis=0, keepdims=True) for j in range(4)]
        + [jnp.zeros((toks - 8, toks), F32)],
        axis=0,
    ).T
    home[...] = tall
    lane = lax.broadcasted_iota(jnp.int32, (toks, toks), 1)
    lane_node = (lane % nodes).astype(F32)
    for j in range(4):
        onehot[j] = jnp.where((lane < 3 * nodes) & (tall[:, j:j + 1] == lane_node), 1.0, 0.0).astype(BF16)

    pl.semaphore_wait(barrier, total - 1)

    def unit(u):
        k0, c0 = u // chunks, u % chunks
        v = u - chunks
        mixed = ((z == 1) | (z == 2)) & (k0 >= 1) & (k0 <= 2)
        k = jnp.where(mixed, 1 + v % 2, k0)
        ch = jnp.where(mixed, v // 2, c0)
        near = z + 1 - 2 * (z % 2)
        low = z < 2
        zb = jnp.where(
            k == 0, z, jnp.where(k == 1, near, jnp.where(k == 2, jnp.where(low, 2, 1), jnp.where(low, 3, 0)))
        )
        return k, ch, zb

    def mate(d):
        return (x + d % 2) % 2 + 2 * ((y + d // 2) % 2)

    def along(ref, index, send, recv, step):
        return pltpu.make_async_remote_copy(
            src_ref=ref.at[index], dst_ref=ref.at[index], send_sem=send.at[index], recv_sem=recv.at[index],
            device_id=(node + step * SIDE, core), device_id_type=MESH,
        )

    def hop(zb, ch, step):
        return along(zbuf, (zb, ch), z_up if step > 0 else z_down, z_recv, step)

    def hop_aux(zb, step):
        return along(aux, zb, a_up if step > 0 else a_down, a_recv, step)

    def pack(zb, ch, d):
        return pltpu.make_async_remote_copy(
            src_ref=sbuf.at[zb, ch, d - 1], dst_ref=rbuf.at[core, ch, zb, q],
            send_sem=r_send.at[zb, ch, d - 1], recv_sem=r_recv.at[zb, ch, d - 1],
            device_id=(z * SIDE + mate(d), core), device_id_type=MESH,
        )

    def pack_in(zb, ch, d):
        return pltpu.make_async_remote_copy(
            src_ref=sbuf.at[zb, ch, d - 1], dst_ref=rbuf.at[core, ch, zb, mate(d)],
            send_sem=r_send.at[zb, ch, d - 1], recv_sem=r_recv.at[zb, ch, d - 1],
            device_id=(z * SIDE + mate(d), core), device_id_type=MESH,
        )

    def scale(zb, d):
        return pltpu.make_async_remote_copy(
            src_ref=psend.at[zb, d - 1], dst_ref=pbuf.at[zb, q],
            send_sem=p_send.at[zb, d - 1], recv_sem=p_recv.at[zb, d - 1],
            device_id=(z * SIDE + mate(d), core), device_id_type=MESH,
        )

    def scale_in(zb, d):
        return pltpu.make_async_remote_copy(
            src_ref=psend.at[zb, d - 1], dst_ref=pbuf.at[zb, mate(d)],
            send_sem=p_send.at[zb, d - 1], recv_sem=p_recv.at[zb, d - 1],
            device_id=(z * SIDE + mate(d), core), device_id_type=MESH,
        )

    def share(half, zb, ch):
        return pltpu.make_async_remote_copy(
            src_ref=rbuf.at[half, ch, zb], dst_ref=rbuf.at[half, ch, zb],
            send_sem=s_send.at[zb, ch], recv_sem=s_recv.at[zb, ch],
            device_id=(node, other), device_id_type=MESH,
        )

    def give(zb, d, dc):
        target = zb * SIDE + mate(d)
        return pltpu.make_async_remote_copy(
            src_ref=part.at[zb, d], dst_ref=ret.at[node, core],
            send_sem=t_send.at[zb, d, dc], recv_sem=t_recv.at[node, core],
            device_id=(target, (core + dc) % 2), device_id_type=MESH,
        )

    def give_in(m, c):
        return pltpu.make_async_remote_copy(
            src_ref=part.at[0, 0], dst_ref=ret.at[m, c],
            send_sem=t_send.at[0, 0, 0], recv_sem=t_recv.at[m, c],
            device_id=(node, other), device_id_type=MESH,
        )

    def store(zb, e):
        return pltpu.make_async_copy(obuf.at[zb, e], out_ref.at[e, zb], o_sem.at[zb, e])

    cap_rows = lax.broadcasted_iota(jnp.int32, (cap, toks), 0).astype(F32)
    cap_lane = lax.broadcasted_iota(jnp.int32, (cap, 128), 1)

    def stage_a(u):
        k, ch, zb = unit(u)

        @pl.when(k == 0)
        def _():
            load_in(ch).wait()

        @pl.when(k > 0)
        def _():
            @pl.when(ch == 0)
            def _():
                hop_aux(zb, 1).wait_recv()

            hop(zb, ch, 1).wait_recv()

        for step, go in ((1, (zb <= z) & (z < PLANES - 1)), (-1, (zb >= z) & (z > 0))):
            @pl.when(go)
            def _(step=step):
                @pl.when(ch == 0)
                def _():
                    hop_aux(zb, step).start()

                hop(zb, ch, step).start()

        @pl.when(ch == 0)
        def _():
            auxf[...] = aux[zb].astype(F32)
            for d in (3, 1, 2, 0):
                m = z * SIDE + mate(d)
                sel = (auxf[pl.ds(m, 1), :] == cap_rows).astype(F32)
                smat[zb, d] = sel.astype(BF16)
                col0 = jnp.sum(sel * auxf[pl.ds(nodes + m, 1), :], axis=1, keepdims=True)
                col1 = jnp.sum(sel * auxf[pl.ds(2 * nodes + m, 1), :], axis=1, keepdims=True)
                value = jnp.where(cap_lane == 0, col0, jnp.where(cap_lane == 1, col1, 0.0)).astype(BF16)
                if d:
                    psend[zb, d - 1] = value
                    scale(zb, d).start()
                else:
                    pbuf[zb, q] = value

        packs = jnp.dot(
            smat[zb].reshape(SIDE * cap, toks), zbuf[zb, ch], preferred_element_type=F32
        ).astype(BF16)
        for d in (3, 1, 2, 0):
            value = packs[d * cap:(d + 1) * cap]
            if d:
                sbuf[zb, ch, d - 1] = value
                pack(zb, ch, d).start()
            else:
                rbuf[core, ch, zb, q] = value

    def stage_b(u):
        k, ch, zb = unit(u)
        for d in (1, 2, 3):
            pack_in(zb, ch, d).wait_recv()

        share(core, zb, ch).start()

    def stage_c(u):
        k, ch, zb = unit(u)
        share(other, zb, ch).wait_recv()

        @pl.when(ch == 0)
        def _():
            acc[zb] = jnp.zeros(acc.shape[1:], F32)

        rows_in = jnp.concatenate(
            [rbuf[h, ch, zb].reshape(SIDE * cap, width) for h in range(2)], axis=1
        )
        tile = min(256, hid)
        for n in range(2 * hid // tile):
            cols = slice(n * tile, (n + 1) * tile)
            acc[zb, :, cols] += lax.dot_general(rows_in, wv[ch, cols, :], NT, preferred_element_type=F32)

        @pl.when(ch == chunks - 1)
        def _():
            for d in (1, 2, 3):
                scale_in(zb, d).wait_recv()
            scales = pbuf[zb].reshape(SIDE * cap, 128).astype(F32)
            folded = []
            for e in range(2):
                g = acc[zb, :, e * hid:(e + 1) * hid]
                prod = hv[e, zb].astype(F32) * g
                fold = prod[:, :128]
                for b in range(1, hid // 128):
                    fold = fold + prod[:, b * 128:(b + 1) * 128]
                folded.append(fold)
                obuf[zb, e] = (scales[:, e:e + 1] * g).astype(BF16)
                store(zb, e).start()
            fill = jnp.zeros((128 - 2 * cap, 128), F32)
            for s in range(SIDE):
                rows = slice(s * cap, (s + 1) * cap)
                sums = jnp.sum(
                    jnp.concatenate([folded[0][rows], folded[1][rows], fill], axis=0).T, axis=0, keepdims=True
                )
                for d in range(SIDE):
                    @pl.when(mate(d) == s)
                    def _(d=d, sums=sums):
                        part[zb, d] = jnp.broadcast_to(sums, (8, 128))
            for d in range(SIDE):
                for dc in range(2):
                    if d == 0 and dc == 0:
                        @pl.when(zb != z)
                        def _():
                            give(zb, 0, 0).start()

                        @pl.when(zb == z)
                        def _():
                            ret[node, core] = part[zb, 0]
                    else:
                        give(zb, d, dc).start()

    far = 2 * chunks + 2
    between = (z == 1) | (z == 2)
    lag = jnp.where(between, far, 2)

    def body(it, carry):
        @pl.when(it < units)
        def _():
            stage_a(it)

        @pl.when(it == 2)
        def _():
            for ch in range(chunks):
                for h in range(2):
                    load_w(h, ch).wait()
            load_h.wait()

        @pl.when((it >= lag) & (it < units + lag))
        def _():
            stage_c(it - lag)

        @pl.when((it >= 1) & (it <= units))
        def _():
            stage_b(it - 1)

        return carry

    lax.fori_loop(0, units + jnp.where(between, far, 2), body, 0)

    def finish_block(zb, carry):
        for e in range(2):
            store(zb, e).wait()
        for step, go in ((1, (zb <= z) & (z < PLANES - 1)), (-1, (zb >= z) & (z > 0))):
            @pl.when(go)
            def _(step=step):
                hop_aux(zb, step).wait_send()

        for d in range(1, SIDE):
            scale(zb, d).wait_send()
        for d in range(SIDE):
            for dc in range(2):
                if d == 0 and dc == 0:
                    @pl.when(zb != z)
                    def _():
                        give(zb, 0, 0).wait_send()
                else:
                    give(zb, d, dc).wait_send()

        def finish_unit(ch, inner):
            for step, go in ((1, (zb <= z) & (z < PLANES - 1)), (-1, (zb >= z) & (z > 0))):
                @pl.when(go)
                def _(step=step):
                    hop(zb, ch, step).wait_send()

            for d in range(1, SIDE):
                pack(zb, ch, d).wait_send()
            share(core, zb, ch).wait_send()
            return inner

        return lax.fori_loop(0, chunks, finish_unit, carry)

    lax.fori_loop(0, PLANES, finish_block, 0)

    def arrive(i, carry):
        peer = (me + i) % total
        give_in(peer // 2, peer % 2).wait_recv()
        return carry

    lax.fori_loop(1, total, arrive, 0)

    sub = lax.broadcasted_iota(jnp.int32, (8, 128), 0)
    halves = []
    for base in range(0, nodes, 8):
        rows = jnp.zeros((8, 128), F32)
        for m in range(8):
            rows = jnp.where(sub == m, ret[base + m, 0] + ret[base + m, 1], rows)
        halves.append(rows)
    sums = jnp.concatenate(halves, axis=0)
    high = sums.astype(BF16).astype(F32)
    rest = sums - high
    middle = rest.astype(BF16).astype(F32)
    parts = jnp.concatenate(
        [high, middle, rest - middle, jnp.zeros((128 - 3 * nodes, 128), F32)], axis=0
    ).astype(BF16)
    lanes = lax.broadcasted_iota(jnp.int32, (toks, 128), 1)
    lanes_f = lanes.astype(F32)
    result = jnp.zeros((toks, 128), F32)
    for j in range(4):
        picked = jnp.dot(onehot[j], parts, preferred_element_type=F32)
        slot = home[:, 4 + j:5 + j]
        for e in range(2):
            column = jnp.sum(jnp.where(lanes_f == slot + float(e * cap), picked, 0.0), axis=1, keepdims=True)
            result = jnp.where(lanes == 2 * j + e, column, result)
    gp_ref[...] = result.T[:8, :]


def fused(chunks, grad_out, probs, node_list, weight_down, saved_hidden):
    toks, half = grad_out.shape
    width = half // chunks
    experts, hid, full = weight_down.shape
    slots = saved_hidden.shape[1]
    cap = slots // (PLANES * SIDE)
    group = SIDE * cap
    dma = pltpu.SemaphoreType.DMA
    anywhere = pl.BlockSpec(memory_space=pl.ANY)
    vmem = pl.BlockSpec(memory_space=pltpu.VMEM)
    out, gp = pl.pallas_call(
        functools.partial(fused_kernel, chunks),
        out_shape=(
            jax.ShapeDtypeStruct((experts, PLANES, group, hid), BF16),
            jax.ShapeDtypeStruct((8, toks), F32),
        ),
        in_specs=[anywhere, vmem, vmem, anywhere, anywhere],
        out_specs=(anywhere, vmem),
        scratch_shapes=[
            pltpu.VMEM((PLANES, chunks, toks, width), BF16),
            pltpu.VMEM((PLANES, 48, toks), BF16),
            pltpu.VMEM((48, toks), F32),
            pltpu.VMEM((PLANES, SIDE, cap, toks), BF16),
            pltpu.VMEM((PLANES, chunks, 3, cap, width), BF16),
            pltpu.VMEM((PLANES, 3, cap, 128), BF16),
            pltpu.VMEM((2, chunks, PLANES, SIDE, cap, width), BF16),
            pltpu.VMEM((PLANES, SIDE, cap, 128), BF16),
            pltpu.VMEM((chunks, experts * hid, 2 * width), BF16),
            pltpu.VMEM((experts, PLANES, group, hid), BF16),
            pltpu.VMEM((PLANES, group, experts * hid), F32),
            pltpu.VMEM((PLANES, experts, group, hid), BF16),
            pltpu.VMEM((PLANES, SIDE, 8, 128), F32),
            pltpu.VMEM((PLANES * SIDE, 2, 8, 128), F32),
            pltpu.VMEM((toks, toks), F32),
            pltpu.VMEM((4, toks, toks), BF16),
            dma((chunks,)),
            dma((2, chunks)),
            dma(()),
            dma((PLANES, 2)),
            dma((PLANES, chunks)),
            dma((PLANES, chunks)),
            dma((PLANES, chunks)),
            dma((PLANES,)),
            dma((PLANES,)),
            dma((PLANES,)),
            dma((PLANES, chunks, 3)),
            dma((PLANES, chunks, 3)),
            dma((PLANES, 3)),
            dma((PLANES, 3)),
            dma((PLANES, chunks)),
            dma((PLANES, chunks)),
            dma((PLANES, SIDE, 2)),
            dma((PLANES * SIDE, 2)),
        ],
        compiler_params=pltpu.CompilerParams(
            collective_id=0, has_side_effects=True, vmem_limit_bytes=56 * 2**20
        ),
        cost_estimate=pl.CostEstimate(
            flops=2 * slots * full * experts * hid, bytes_accessed=2 * experts * hid * full, transcendentals=0
        ),
    )(
        grad_out,
        probs.T,
        node_list.T,
        weight_down.reshape(experts * hid, full),
        saved_hidden.reshape(experts, PLANES, group, hid),
    )
    return out.reshape(experts, slots, hid), gp.T


def on_device(*args):
    grad_out, probs, node_list, weight_down, saved_hidden = args
    nodes, cores = lax.axis_size("node"), lax.axis_size("local")
    cap = saved_hidden.shape[1] // nodes
    suits = (
        nodes == PLANES * SIDE
        and cores == 2
        and cap % 16 == 0
        and 2 * cap <= 128
        and node_list.shape == (128, 4)
        and weight_down.shape[0] == 2
        and weight_down.shape[1] % 128 == 0
        and grad_out.shape[1] % 512 == 0
    )
    if suits:
        return fused(4, *args)
    return plain(*args)


def solution(mesh):
    return jax.shard_map(
        on_device,
        mesh=mesh,
        in_specs=(
            P("node", "local"),
            P("node", None),
            P("node", None),
            P("node", "local", None),
            P("node", None, "local"),
        ),
        out_specs=(P("node", None, "local"), P("node", None)),
        check_vma=False,
    )
```

```python
import functools

import jax
import jax.numpy as jnp
from jax import lax
from jax.experimental import pallas as pl
from jax.experimental.pallas import tpu as pltpu
from jax.sharding import PartitionSpec as P

MESH = pl.DeviceIdType.MESH
PLANES = 4
SIDE = 4
F32 = jnp.float32
BF16 = jnp.bfloat16
NT = (((1,), (1,)), ((), ()))


def gather_slots(source, source_row, slot_valid):
    padded = jnp.concatenate([source, jnp.zeros((1, source.shape[1]), source.dtype)], axis=0)
    index = jnp.where(slot_valid, source_row, source.shape[0])
    return jnp.take(padded, index, axis=0)


def plain(grad_out, probs, node_list, weight_down, saved_hidden):
    node_count = lax.axis_size("node")
    tok_rows = node_list.shape[0]
    route_count = node_list.shape[1]
    slot_rows = saved_hidden.shape[1]
    capacity = slot_rows // node_count
    expert_count = weight_down.shape[0]
    node_ids = lax.broadcasted_iota(jnp.int32, (tok_rows, route_count, node_count), 2)
    listed = (node_list[:, :, None] == node_ids).astype(jnp.float32)
    member = jnp.sum((node_list[:, :, None] == node_ids).astype(jnp.int32), axis=1)
    arrival = jnp.cumsum(member, axis=0) - member
    positions = lax.broadcasted_iota(jnp.int32, (tok_rows, node_count, capacity), 2)
    select_mask = (arrival[:, :, None] == positions) & (member[:, :, None] == 1)
    select_count = select_mask.astype(jnp.int32)
    token_iota = lax.broadcasted_iota(jnp.int32, (tok_rows, node_count, capacity), 0)
    source_row = jnp.sum(select_count * token_iota, axis=0)
    slot_valid = jnp.sum(select_count, axis=0) > 0
    select_full = select_mask.astype(jnp.float32)
    grouped = probs.reshape(tok_rows, route_count, expert_count).astype(jnp.float32)
    picked = jnp.einsum("tjm,tjc->tmc", listed, grouped, precision=lax.Precision.HIGHEST)
    prob_send = jnp.einsum(
        "tms,tmc->msc", select_full, picked, precision=lax.Precision.HIGHEST
    ).astype(jnp.bfloat16)
    rows_send = gather_slots(grad_out, source_row, slot_valid)
    rows_in, prob_in = (
        lax.all_to_all(rows_send, "node", split_axis=0, concat_axis=0, tiled=True),
        lax.all_to_all(prob_send, "node", split_axis=0, concat_axis=0, tiled=True),
    )
    rows_in = lax.all_gather(rows_in.reshape(slot_rows, -1), "local", axis=1, tiled=True)
    hidden_grads = jnp.einsum(
        "rd,ehd->erh", rows_in, weight_down, preferred_element_type=jnp.float32
    )
    scales = jnp.transpose(prob_in.reshape(slot_rows, expert_count).astype(jnp.float32))
    grad_hidden = (scales[:, :, None] * hidden_grads).astype(jnp.bfloat16)
    partial_value = jnp.sum(saved_hidden.astype(jnp.float32) * hidden_grads, axis=2)
    partial_value = jnp.transpose(partial_value).reshape(node_count, capacity, expert_count)
    summed = lax.psum(partial_value, "local")
    returned = lax.all_to_all(summed, "node", split_axis=0, concat_axis=0, tiled=True)
    per_node = jnp.einsum("tms,msc->tmc", select_full, returned, precision=lax.Precision.HIGHEST)
    grad_probs = jnp.einsum("tjm,tmc->tjc", listed, per_node, precision=lax.Precision.HIGHEST)
    return (grad_hidden, grad_probs.reshape(tok_rows, route_count * expert_count))


def fused_kernel(
    chunks, go_ref, pr_ref, nl_ref, w_ref, sh_ref, out_ref, gp_ref,
    zbuf, aux, auxf, smat, sbuf, psend, rbuf, pbuf, wv, hv, acc, obuf, part, ret, home, onehot,
    in_sem, w_sem, h_sem, o_sem, z_recv, z_up, z_down, a_recv, a_up, a_down,
    r_send, r_recv, p_send, p_recv, s_send, s_recv, t_send, t_recv,
):
    node, core = lax.axis_index("node"), lax.axis_index("local")
    z, q = node // SIDE, node % SIDE
    x, y = q % 2, q // 2
    cap, width = rbuf.shape[4], rbuf.shape[5]
    toks = zbuf.shape[2]
    hid = hv.shape[3]
    units = PLANES * chunks
    other = 1 - core
    total = PLANES * SIDE * 2
    me = node * 2 + core

    barrier = pltpu.get_barrier_semaphore()

    def greet(i, carry):
        peer = (me + i) % total
        pl.semaphore_signal(barrier, inc=1, device_id=(peer // 2, peer % 2), device_id_type=MESH)
        return carry

    lax.fori_loop(1, total, greet, 0)

    def load_in(ch):
        return pltpu.make_async_copy(go_ref.at[:, pl.ds(ch * width, width)], zbuf.at[z, ch], in_sem.at[ch])

    def load_w(h, ch):
        return pltpu.make_async_copy(
            w_ref.at[:, pl.ds((h * chunks + ch) * width, width)], wv.at[ch, :, pl.ds(h * width, width)],
            w_sem.at[h, ch],
        )

    load_h = pltpu.make_async_copy(sh_ref, hv, h_sem)
    for ch in range(chunks):
        load_in(ch).start()
    for ch in range(chunks):
        for h in range(2):
            load_w(h, ch).start()
    load_h.start()

    nodes = PLANES * SIDE
    rows_m = lax.broadcasted_iota(jnp.int32, (nodes, toks), 0)
    member = jnp.zeros((nodes, toks), F32)
    first = jnp.zeros((nodes, toks), F32)
    second = jnp.zeros((nodes, toks), F32)
    hits = []
    for j in range(4):
        hit = (nl_ref[j:j + 1, :] == rows_m).astype(F32)
        hits.append(hit)
        member = member + hit
        first = first + hit * pr_ref[2 * j:2 * j + 1, :].astype(F32)
        second = second + hit * pr_ref[2 * j + 1:2 * j + 2, :].astype(F32)
    before = (
        lax.broadcasted_iota(jnp.int32, (toks, toks), 0) < lax.broadcasted_iota(jnp.int32, (toks, toks), 1)
    ).astype(F32).astype(BF16)
    arrival = jnp.dot(member.astype(BF16), before, preferred_element_type=F32)
    slot_of = jnp.where(member > 0.5, arrival, -1.0)
    aux[z] = jnp.concatenate([slot_of, first, second], axis=0).astype(BF16)
    tall = jnp.concatenate(
        [nl_ref[...].astype(F32)]
        + [jnp.sum(hits[j] * slot_of, axis=0, keepdims=True) for j in range(4)]
        + [jnp.zeros((toks - 8, toks), F32)],
        axis=0,
    ).T
    home[...] = tall
    lane = lax.broadcasted_iota(jnp.int32, (toks, toks), 1)
    lane_node = (lane % nodes).astype(F32)
    for j in range(4):
        onehot[j] = jnp.where((lane < 3 * nodes) & (tall[:, j:j + 1] == lane_node), 1.0, 0.0).astype(BF16)

    pl.semaphore_wait(barrier, total - 1)

    def block(k):
        near = z + 1 - 2 * (z % 2)
        low = z < 2
        return jnp.where(
            k == 0, z, jnp.where(k == 1, near, jnp.where(k == 2, jnp.where(low, 2, 1), jnp.where(low, 3, 0)))
        )

    def unit(u):
        k0, c0 = u // chunks, u % chunks
        v = u - chunks
        mixed = ((z == 1) | (z == 2)) & (k0 >= 1) & (k0 <= 2)
        k = jnp.where(mixed, 1 + v % 2, k0)
        ch = jnp.where(mixed, v // 2, c0)
        return k, ch, block(k)

    def mate(d):
        return (x + d % 2) % 2 + 2 * ((y + d // 2) % 2)

    def along(ref, index, send, recv, step):
        return pltpu.make_async_remote_copy(
            src_ref=ref.at[index], dst_ref=ref.at[index], send_sem=send.at[index], recv_sem=recv.at[index],
            device_id=(node + step * SIDE, core), device_id_type=MESH,
        )

    def hop(zb, ch, step):
        return along(zbuf, (zb, ch), z_up if step > 0 else z_down, z_recv, step)

    def hop_aux(zb, step):
        return along(aux, zb, a_up if step > 0 else a_down, a_recv, step)

    def pack(zb, ch, d):
        return pltpu.make_async_remote_copy(
            src_ref=sbuf.at[zb, ch, d - 1], dst_ref=rbuf.at[core, ch, zb, q],
            send_sem=r_send.at[zb, ch, d - 1], recv_sem=r_recv.at[zb, ch, d - 1],
            device_id=(z * SIDE + mate(d), core), device_id_type=MESH,
        )

    def pack_in(zb, ch, d):
        return pltpu.make_async_remote_copy(
            src_ref=sbuf.at[zb, ch, d - 1], dst_ref=rbuf.at[core, ch, zb, mate(d)],
            send_sem=r_send.at[zb, ch, d - 1], recv_sem=r_recv.at[zb, ch, d - 1],
            device_id=(z * SIDE + mate(d), core), device_id_type=MESH,
        )

    def scale(zb, d):
        return pltpu.make_async_remote_copy(
            src_ref=psend.at[zb, d - 1], dst_ref=pbuf.at[zb, q],
            send_sem=p_send.at[zb, d - 1], recv_sem=p_recv.at[zb, d - 1],
            device_id=(z * SIDE + mate(d), core), device_id_type=MESH,
        )

    def scale_in(zb, d):
        return pltpu.make_async_remote_copy(
            src_ref=psend.at[zb, d - 1], dst_ref=pbuf.at[zb, mate(d)],
            send_sem=p_send.at[zb, d - 1], recv_sem=p_recv.at[zb, d - 1],
            device_id=(z * SIDE + mate(d), core), device_id_type=MESH,
        )

    def share(half, zb, ch):
        return pltpu.make_async_remote_copy(
            src_ref=rbuf.at[half, ch, zb], dst_ref=rbuf.at[half, ch, zb],
            send_sem=s_send.at[zb, ch], recv_sem=s_recv.at[zb, ch],
            device_id=(node, other), device_id_type=MESH,
        )

    def give(zb, d, dc):
        target = zb * SIDE + mate(d)
        return pltpu.make_async_remote_copy(
            src_ref=part.at[zb, d], dst_ref=ret.at[node, core],
            send_sem=t_send.at[zb, d, dc], recv_sem=t_recv.at[node, core],
            device_id=(target, (core + dc) % 2), device_id_type=MESH,
        )

    def give_in(m, c):
        return pltpu.make_async_remote_copy(
            src_ref=part.at[0, 0], dst_ref=ret.at[m, c],
            send_sem=t_send.at[0, 0, 0], recv_sem=t_recv.at[m, c],
            device_id=(node, other), device_id_type=MESH,
        )

    def store(zb, e):
        return pltpu.make_async_copy(obuf.at[zb, e], out_ref.at[e, zb], o_sem.at[zb, e])

    cap_rows = lax.broadcasted_iota(jnp.int32, (cap, toks), 0).astype(F32)
    cap_lane = lax.broadcasted_iota(jnp.int32, (cap, 128), 1)

    def stage_a(u):
        k, ch, zb = unit(u)

        @pl.when(k == 0)
        def _():
            load_in(ch).wait()

        @pl.when(k > 0)
        def _():
            @pl.when(ch == 0)
            def _():
                hop_aux(zb, 1).wait_recv()

            hop(zb, ch, 1).wait_recv()

        for step, go in ((1, (zb <= z) & (z < PLANES - 1)), (-1, (zb >= z) & (z > 0))):
            @pl.when(go)
            def _(step=step):
                @pl.when(ch == 0)
                def _():
                    hop_aux(zb, step).start()

                hop(zb, ch, step).start()

        @pl.when(ch == 0)
        def _():
            auxf[...] = aux[zb].astype(F32)
            for d in (3, 1, 2, 0):
                m = z * SIDE + mate(d)
                sel = (auxf[pl.ds(m, 1), :] == cap_rows).astype(F32)
                smat[zb, d] = sel.astype(BF16)
                col0 = jnp.sum(sel * auxf[pl.ds(nodes + m, 1), :], axis=1, keepdims=True)
                col1 = jnp.sum(sel * auxf[pl.ds(2 * nodes + m, 1), :], axis=1, keepdims=True)
                value = jnp.where(cap_lane == 0, col0, jnp.where(cap_lane == 1, col1, 0.0)).astype(BF16)
                if d:
                    psend[zb, d - 1] = value
                    scale(zb, d).start()
                else:
                    pbuf[zb, q] = value

        packs = jnp.dot(
            smat[zb].reshape(SIDE * cap, toks), zbuf[zb, ch], preferred_element_type=F32
        ).astype(BF16)
        for d in (3, 1, 2, 0):
            value = packs[d * cap:(d + 1) * cap]
            if d:
                sbuf[zb, ch, d - 1] = value
                pack(zb, ch, d).start()
            else:
                rbuf[core, ch, zb, q] = value

    def stage_b(u):
        k, ch, zb = unit(u)
        for d in (1, 2, 3):
            pack_in(zb, ch, d).wait_recv()

        share(core, zb, ch).start()

    def stage_c(u):
        k, ch, zb = unit(u)
        share(other, zb, ch).wait_recv()

        @pl.when(ch == 0)
        def _():
            acc[zb] = jnp.zeros(acc.shape[1:], F32)

        rows_in = jnp.concatenate(
            [rbuf[h, ch, zb].reshape(SIDE * cap, width) for h in range(2)], axis=1
        )
        tile = min(256, hid)
        for n in range(2 * hid // tile):
            cols = slice(n * tile, (n + 1) * tile)
            acc[zb, :, cols] += lax.dot_general(rows_in, wv[ch, cols, :], NT, preferred_element_type=F32)

        @pl.when(ch == chunks - 1)
        def _():
            for d in (1, 2, 3):
                scale_in(zb, d).wait_recv()
            scales = pbuf[zb].reshape(SIDE * cap, 128).astype(F32)
            folded = []
            for e in range(2):
                g = acc[zb, :, e * hid:(e + 1) * hid]
                prod = hv[e, zb].astype(F32) * g
                fold = prod[:, :128]
                for b in range(1, hid // 128):
                    fold = fold + prod[:, b * 128:(b + 1) * 128]
                folded.append(fold)
                obuf[zb, e] = (scales[:, e:e + 1] * g).astype(BF16)
                store(zb, e).start()
            fill = jnp.zeros((128 - 2 * cap, 128), F32)
            for s in range(SIDE):
                rows = slice(s * cap, (s + 1) * cap)
                sums = jnp.sum(
                    jnp.concatenate([folded[0][rows], folded[1][rows], fill], axis=0).T, axis=0, keepdims=True
                )
                for d in range(SIDE):
                    @pl.when(mate(d) == s)
                    def _(d=d, sums=sums):
                        part[zb, d] = jnp.broadcast_to(sums, (8, 128))
            for d in range(SIDE):
                for dc in range(2):
                    if d == 0 and dc == 0:
                        @pl.when(zb != z)
                        def _():
                            give(zb, 0, 0).start()

                        @pl.when(zb == z)
                        def _():
                            ret[node, core] = part[zb, 0]
                    else:
                        give(zb, d, dc).start()

    def finish_block(k, carry):
        zb = block(k)
        for e in range(2):
            store(zb, e).wait()
        for step, go in ((1, (zb <= z) & (z < PLANES - 1)), (-1, (zb >= z) & (z > 0))):
            @pl.when(go)
            def _(step=step):
                hop_aux(zb, step).wait_send()

        for d in range(1, SIDE):
            scale(zb, d).wait_send()
        for d in range(SIDE):
            for dc in range(2):
                if d == 0 and dc == 0:
                    @pl.when(zb != z)
                    def _():
                        give(zb, 0, 0).wait_send()
                else:
                    give(zb, d, dc).wait_send()

        def finish_unit(ch, inner):
            for step, go in ((1, (zb <= z) & (z < PLANES - 1)), (-1, (zb >= z) & (z > 0))):
                @pl.when(go)
                def _(step=step):
                    hop(zb, ch, step).wait_send()

            for d in range(1, SIDE):
                pack(zb, ch, d).wait_send()
            share(core, zb, ch).wait_send()
            return inner

        return lax.fori_loop(0, chunks, finish_unit, carry)

    between = (z == 1) | (z == 2)
    swap = jnp.where(between, chunks // 2 + 1, 1)
    lag = jnp.where(between, chunks + 1, 2)

    def body(it, carry):
        @pl.when(it == units + lag - 3)
        def _():
            lax.fori_loop(0, 2, finish_block, 0)

        @pl.when(it < units)
        def _():
            stage_a(it)

        @pl.when(it == 2)
        def _():
            for ch in range(chunks):
                for h in range(2):
                    load_w(h, ch).wait()
            load_h.wait()

        @pl.when((it >= lag) & (it < units + lag))
        def _():
            stage_c(it - lag)

        @pl.when((it >= swap) & (it < units + swap))
        def _():
            stage_b(it - swap)

        return carry

    lax.fori_loop(0, units + lag, body, 0)

    lax.fori_loop(2, PLANES, finish_block, 0)

    def arrive(i, carry):
        peer = (me + i) % total
        give_in(peer // 2, peer % 2).wait_recv()
        return carry

    lax.fori_loop(1, total, arrive, 0)

    sub = lax.broadcasted_iota(jnp.int32, (8, 128), 0)
    halves = []
    for base in range(0, nodes, 8):
        rows = jnp.zeros((8, 128), F32)
        for m in range(8):
            rows = jnp.where(sub == m, ret[base + m, 0] + ret[base + m, 1], rows)
        halves.append(rows)
    sums = jnp.concatenate(halves, axis=0)
    high = sums.astype(BF16).astype(F32)
    rest = sums - high
    middle = rest.astype(BF16).astype(F32)
    parts = jnp.concatenate(
        [high, middle, rest - middle, jnp.zeros((128 - 3 * nodes, 128), F32)], axis=0
    ).astype(BF16)
    lanes = lax.broadcasted_iota(jnp.int32, (toks, 128), 1)
    lanes_f = lanes.astype(F32)
    result = jnp.zeros((toks, 128), F32)
    for j in range(4):
        picked = jnp.dot(onehot[j], parts, preferred_element_type=F32)
        slot = home[:, 4 + j:5 + j]
        for e in range(2):
            column = jnp.sum(jnp.where(lanes_f == slot + float(e * cap), picked, 0.0), axis=1, keepdims=True)
            result = jnp.where(lanes == 2 * j + e, column, result)
    gp_ref[...] = result.T[:8, :]


def fused(chunks, grad_out, probs, node_list, weight_down, saved_hidden):
    toks, half = grad_out.shape
    width = half // chunks
    experts, hid, full = weight_down.shape
    slots = saved_hidden.shape[1]
    cap = slots // (PLANES * SIDE)
    group = SIDE * cap
    dma = pltpu.SemaphoreType.DMA
    anywhere = pl.BlockSpec(memory_space=pl.ANY)
    vmem = pl.BlockSpec(memory_space=pltpu.VMEM)
    out, gp = pl.pallas_call(
        functools.partial(fused_kernel, chunks),
        out_shape=(
            jax.ShapeDtypeStruct((experts, PLANES, group, hid), BF16),
            jax.ShapeDtypeStruct((8, toks), F32),
        ),
        in_specs=[anywhere, vmem, vmem, anywhere, anywhere],
        out_specs=(anywhere, vmem),
        scratch_shapes=[
            pltpu.VMEM((PLANES, chunks, toks, width), BF16),
            pltpu.VMEM((PLANES, 48, toks), BF16),
            pltpu.VMEM((48, toks), F32),
            pltpu.VMEM((PLANES, SIDE, cap, toks), BF16),
            pltpu.VMEM((PLANES, chunks, 3, cap, width), BF16),
            pltpu.VMEM((PLANES, 3, cap, 128), BF16),
            pltpu.VMEM((2, chunks, PLANES, SIDE, cap, width), BF16),
            pltpu.VMEM((PLANES, SIDE, cap, 128), BF16),
            pltpu.VMEM((chunks, experts * hid, 2 * width), BF16),
            pltpu.VMEM((experts, PLANES, group, hid), BF16),
            pltpu.VMEM((PLANES, group, experts * hid), F32),
            pltpu.VMEM((PLANES, experts, group, hid), BF16),
            pltpu.VMEM((PLANES, SIDE, 8, 128), F32),
            pltpu.VMEM((PLANES * SIDE, 2, 8, 128), F32),
            pltpu.VMEM((toks, toks), F32),
            pltpu.VMEM((4, toks, toks), BF16),
            dma((chunks,)),
            dma((2, chunks)),
            dma(()),
            dma((PLANES, 2)),
            dma((PLANES, chunks)),
            dma((PLANES, chunks)),
            dma((PLANES, chunks)),
            dma((PLANES,)),
            dma((PLANES,)),
            dma((PLANES,)),
            dma((PLANES, chunks, 3)),
            dma((PLANES, chunks, 3)),
            dma((PLANES, 3)),
            dma((PLANES, 3)),
            dma((PLANES, chunks)),
            dma((PLANES, chunks)),
            dma((PLANES, SIDE, 2)),
            dma((PLANES * SIDE, 2)),
        ],
        compiler_params=pltpu.CompilerParams(
            collective_id=0, has_side_effects=True, vmem_limit_bytes=56 * 2**20
        ),
        cost_estimate=pl.CostEstimate(
            flops=2 * slots * full * experts * hid, bytes_accessed=2 * experts * hid * full, transcendentals=0
        ),
    )(
        grad_out,
        probs.T,
        node_list.T,
        weight_down.reshape(experts * hid, full),
        saved_hidden.reshape(experts, PLANES, group, hid),
    )
    return out.reshape(experts, slots, hid), gp.T


def on_device(*args):
    grad_out, probs, node_list, weight_down, saved_hidden = args
    nodes, cores = lax.axis_size("node"), lax.axis_size("local")
    cap = saved_hidden.shape[1] // nodes
    suits = (
        nodes == PLANES * SIDE
        and cores == 2
        and cap % 16 == 0
        and 2 * cap <= 128
        and node_list.shape == (128, 4)
        and weight_down.shape[0] == 2
        and weight_down.shape[1] % 128 == 0
        and grad_out.shape[1] % (7 * 128) == 0
    )
    if suits:
        return fused(7, *args)
    return plain(*args)


def solution(mesh):
    return jax.shard_map(
        on_device,
        mesh=mesh,
        in_specs=(
            P("node", "local"),
            P("node", None),
            P("node", None),
            P("node", "local", None),
            P("node", None, "local"),
        ),
        out_specs=(P("node", None, "local"), P("node", None)),
        check_vma=False,
    )
```
